32 devices in a mesh: dp: 8 (over y, x, core), tensor: 4 (over z).
Axes of the slice: x: 2, y: 2, z: 4, core: 2. Of those that a mesh axis runs over, the one named last changes fastest.
Arguments:
- inputs: bfloat16 [512, 24, 768], P('tensor', 'dp'), may hold values from -6 to 6
- cotangent: bfloat16 [512, 24, 768], P('tensor', 'dp'), may hold values from -6 to 6
- norm_gain: bfloat16 [2, 2, 768], P(None, None, ('dp', 'tensor')), may hold values from 0.25 to 1.75
- norm_shift: bfloat16 [2, 2, 768], P(None, None, ('dp', 'tensor')), may hold values from -3 to 3
- attention_weight: bfloat16 [2, 3, 768, 768], P(None, None, 'dp', 'tensor'), may hold values from -0.21875 to 0.21875
- attention_bias: bfloat16 [2, 2, 768], P(None, None, ('dp', 'tensor')), may hold values from -3 to 3
- output_weight: bfloat16 [2, 768, 768], P(None, 'tensor', 'dp'), may hold values from -0.875 to 0.875
- output_bias: bfloat16 [2, 768], P(None, ('dp', 'tensor')), may hold values from -3 to 3
- expand_weight: bfloat16 [2, 768, 3072], P(None, 'dp', 'tensor'), may hold values from -0.21875 to 0.21875
- expand_bias: bfloat16 [2, 3072], P(None, ('dp', 'tensor')), may hold values from -3 to 3
- contract_weight: bfloat16 [2, 3072, 768], P(None, 'tensor', 'dp'), may hold values from -0.15625 to 0.15625
- contract_bias: bfloat16 [2, 768], P(None, ('dp', 'tensor')), may hold values from -3 to 3
Outputs:
- outputs: bfloat16 [512, 24, 768], P('tensor', 'dp')
- first_input_gradient: float32 [512, 24, 768], P('tensor', 'dp')
- gain_gradient: float32 [2, 2, 768], P(None, None, ('dp', 'tensor'))
- shift_gradient: float32 [2, 2, 768], P(None, None, ('dp', 'tensor'))
- attention_gradient: float32 [2, 3, 768, 768], P(None, None, 'dp', 'tensor')
- attention_bias_gradient: float32 [2, 2, 768], P(None, None, ('dp', 'tensor'))
- output_gradient: float32 [2, 768, 768], P(None, 'tensor', 'dp')
- output_bias_gradient: float32 [2, 768], P(None, ('dp', 'tensor'))
- expand_gradient: float32 [2, 768, 3072], P(None, 'dp', 'tensor')
- expand_bias_gradient: float32 [2, 3072], P(None, ('dp', 'tensor'))
- contract_gradient: float32 [2, 3072, 768], P(None, 'tensor', 'dp')
- contract_bias_grads: float32 [2, 768], P(None, ('dp', 'tensor'))
The draws below stay inside these ranges and needn't reach their ends.
All inputs are finite; a program needn't handle non-finite values.
Results may differ from the reference program's by a relative error of at most 0.019.
Values may be sent and summed in bfloat16 or wider, within the bound.
A program may use at most 192 MiB of HBM per device.

```python
import math
import jax
import jax.numpy as jnp
from jax import lax

D = 768
HEADS = 12
HEAD = 64
FF = 3072
LEN = 512
LAYERS = 2
SEQS = 24


def spiked(values, rng, source, target, shards_of, factor):
    def block_of(axis_at):
        return (jnp.arange(values.shape[axis_at]) // (values.shape[axis_at] // shards_of)).reshape((-1,) + (1,) * (values.ndim - 1 - axis_at))

    near = jax.random.permutation(rng, shards_of)[block_of(target)]
    far = (block_of(target) + shards_of // 2) % shards_of
    return jnp.where((block_of(source) == near) | (block_of(source) == far), factor * values, values)


def steps_of(stream_key, extent, cuts, least, largest):
    loudness = 1.0
    for position, blocks in cuts:
        draws = jax.random.uniform(jax.random.fold_in(jax.random.fold_in(stream_key, 6), position), (blocks,), jnp.float32, least / len(cuts), largest / len(cuts))
        loudness = loudness * jnp.repeat(jnp.exp(draws), extent[position] // blocks).reshape((-1,) + (1,) * (len(extent) - 1 - position))
    return loudness


def bell_draw(own_key, extent, width, limit, cuts=(), held_as=jnp.bfloat16):
    values = jax.random.normal(own_key, extent, jnp.float32) * width
    if len(cuts) > 0:
        values = steps_of(own_key, extent, cuts, -0.22, 0.18) * values
    return jnp.clip(values, min=-limit, max=limit).astype(held_as)


def gaussian_with(stream_key, extent, scale, bound, pieces, heavy, dtype=jnp.bfloat16):
    values = scale * jax.random.normal(stream_key, extent, jnp.float32)
    if pieces:
        values = values * steps_of(stream_key, extent, pieces, -0.22, 0.18)
    return jnp.clip(spiked(values, jax.random.fold_in(stream_key, 3), *heavy), -bound, bound).astype(dtype)


def setup_inputs(seed: int = 0) -> dict:
    arg_keys = jax.random.split(jax.random.key(seed), 13)
    return {
        "inputs": bell_draw(arg_keys[0], (LEN, SEQS, D), 1.0, 6.0, ((0, 4), (1, 8))),
        "cotangent": gaussian_with(arg_keys[1], (LEN, SEQS, D), 1.0, 6.0, ((0, 4), (1, 8)), (1, 2, 8, 2.0)),
        "norm_gain": jnp.clip(1.0 + 0.15 * jax.random.normal(arg_keys[2], (LAYERS, 2, D), jnp.float32), 0.25, 1.75).astype(jnp.bfloat16),
        "norm_shift": bell_draw(arg_keys[3], (LAYERS, 2, D), 0.5, 3.0, ((2, 32),)),
        "attention_weight": bell_draw(arg_keys[4], (LAYERS, 3, D, D), D ** -0.5, 0.21875, ((2, 8), (3, 4))),
        "attention_bias": bell_draw(arg_keys[5], (LAYERS, 2, D), 0.5, 3.0, ((2, 32),)),
        "output_weight": bell_draw(arg_keys[6], (LAYERS, D, D), (max(D // 16, 8 * D // LEN)) ** -0.5, 0.875, ((1, 4), (2, 8))),
        "output_bias": bell_draw(arg_keys[7], (LAYERS, D), 0.5, 3.0, ((1, 32),)),
        "expand_weight": bell_draw(arg_keys[8], (LAYERS, D, FF), D ** -0.5, 0.21875, ((1, 8), (2, 4))),
        "expand_bias": bell_draw(arg_keys[9], (LAYERS, FF), 0.5, 3.0, ((1, 32),)),
        "contract_weight": bell_draw(arg_keys[10], (LAYERS, FF, D), (FF // 2) ** -0.5, 0.15625, ((1, 4), (2, 8))),
        "contract_bias": bell_draw(arg_keys[11], (LAYERS, D), 0.5, 3.0, ((1, 32),)),
    }


@jax.custom_vjp
def low(v):
    return lax.optimization_barrier(v.astype(jnp.bfloat16)).astype(jnp.float32)

@jax.custom_vjp
def low_back(v):
    return v

def low_keep(v):
    return (low(v), None)

def low_pass(kept, grad):
    return (grad,)

def back_keep(v):
    return (v, None)

def back_low(kept, grad):
    return (low(grad),)
low.defvjp(low_keep, low_pass)
low_back.defvjp(back_keep, back_low)
HIGHEST = lax.Precision.HIGHEST
EPSILON = 1e-05

def normalize(rows, gain, shift):
    average = lax.optimization_barrier(jnp.mean(rows, axis=-1, keepdims=True))
    centred = rows - average
    inverse = lax.rsqrt(lax.optimization_barrier(jnp.mean(centred * centred, axis=-1, keepdims=True)) + EPSILON)
    return centred * inverse * gain + shift

def product(rows, matrix):
    return jnp.einsum('lsd,de->lse', rows, matrix, precision=HIGHEST)

def one_sequence(triple):
    query, keys, values = triple
    length = query.shape[0]
    query = query.reshape(length, HEADS, HEAD)
    keys = keys.reshape(length, HEADS, HEAD)
    values = values.reshape(length, HEADS, HEAD)
    scores = low_back(jnp.einsum('qhd,khd->hqk', query, keys, precision=HIGHEST) * HEAD ** (-0.5))
    causal = jnp.arange(length)[:, None] >= jnp.arange(length)[None, :]
    scores = jnp.where(causal[None], scores, -1e+30)
    weights = low(jax.nn.softmax(scores, axis=-1))
    context = jnp.einsum('hqk,khd->qhd', weights, values, precision=HIGHEST)
    return context.reshape(length, HEADS * HEAD)

def one_layer(rows, params, layer):
    gain, shift, attn_w, attn_b, out_w, out_b, exp_w, exp_b, con_w, con_b = [item[layer] for item in params]
    normed = low(normalize(rows, gain[0], shift[0]))
    query = low(low_back(product(normed, attn_w[0])) + attn_b[0])
    keys = low(low_back(product(normed, attn_w[1])))
    values = low(low_back(product(normed, attn_w[2])) + attn_b[1])
    attend = jax.checkpoint(one_sequence)
    context = lax.map(attend, (query.transpose(1, 0, 2), keys.transpose(1, 0, 2), values.transpose(1, 0, 2)))
    context = low(low_back(context.transpose(1, 0, 2)))
    middle = rows + low_back(product(context, out_w)) + out_b
    expanded = low(normalize(middle, gain[1], shift[1]))
    hidden = low_back(product(expanded, exp_w)) + exp_b
    active_rows = low(jax.nn.gelu(hidden, approximate=True))
    return middle + low_back(product(active_rows, con_w)) + con_b

def reference(inputs, cotangent, norm_gain, norm_shift, attention_weight, attention_bias, output_weight, output_bias, expand_weight, expand_bias, contract_weight, contract_bias):
    params = tuple((item.astype(jnp.float32) for item in (norm_gain, norm_shift, attention_weight, attention_bias, output_weight, output_bias, expand_weight, expand_bias, contract_weight, contract_bias)))
    group = math.gcd(SEQS, 8)
    blocks = SEQS // group

    def split(array):
        return array.astype(jnp.float32).reshape(LEN, blocks, group, D).transpose(1, 0, 2, 3)

    def join(array):
        return array.transpose(1, 0, 2, 3).reshape(LEN, SEQS, D)

    def forward(rows, layer_parameters):
        for layer in range(LAYERS):
            rows = one_layer(rows, layer_parameters, layer)
        return rows

    def add_up(first, second):
        return first + second

    def step(totals, pair):
        rows, upstream = pair
        result, pull = jax.vjp(forward, rows, params)
        grad_rows, grad_params = pull(upstream)
        totals = jax.tree.map(add_up, totals, grad_params)
        return (totals, (result.astype(jnp.bfloat16), grad_rows))
    zeros = jax.tree.map(jnp.zeros_like, params)
    totals, (results, gradients) = lax.scan(step, zeros, (split(inputs), split(cotangent)))
    return (join(results), join(gradients), totals[0], totals[1], totals[2], totals[3], totals[4], totals[5], totals[6], totals[7], totals[8], totals[9])
```

```python
import functools

import jax
import jax.numpy as jnp
from jax import lax
from jax.experimental import pallas as pl
from jax.experimental.pallas import tpu as pltpu
from jax.sharding import PartitionSpec as P

HEAD = 64
EPSILON = 1e-05
ROWS = 256
F32 = jnp.float32
BF16 = jnp.bfloat16


def norm_stats(rows):
    average = jnp.mean(rows, axis=-1, keepdims=True)
    centred = rows - average
    inverse = lax.rsqrt(jnp.mean(centred * centred, axis=-1, keepdims=True) + EPSILON)
    return (centred * inverse, inverse)


def norm_back(incoming, gain, scaled, inverse):
    weighted = incoming * gain
    first = jnp.mean(weighted, axis=-1, keepdims=True)
    second = jnp.mean(weighted * scaled, axis=-1, keepdims=True)
    return inverse * (weighted - first - scaled * second)


def smooth_unit(values):
    return jax.nn.gelu(values, approximate=True)


def dot(left, right, contract):
    return lax.dot_general(left, right, (contract, ((), ())), preferred_element_type=F32)


def block_probs(query, keys, start):
    scores = dot(query, keys, ((1,), (1,)))
    later = lax.broadcasted_iota(jnp.int32, scores.shape, 0) + start
    earlier = lax.broadcasted_iota(jnp.int32, scores.shape, 1)
    scores = jnp.where(later >= earlier, scores, -1e30)
    powers = jnp.exp(scores - jnp.max(scores, axis=-1, keepdims=True))
    return powers / jnp.sum(powers, axis=-1, keepdims=True)


def attend_kernel(qkv_ref, context_ref):
    length = qkv_ref.shape[1]
    for start in range(0, length, ROWS):
        stop = start + ROWS
        parts = []
        for head in range(2):
            lanes = slice(head * HEAD, (head + 1) * HEAD)
            query = qkv_ref[0, start:stop, lanes] * BF16(HEAD**-0.5)
            probs = block_probs(query, qkv_ref[1, :stop, lanes], start)
            parts.append(dot(probs.astype(BF16), qkv_ref[2, :stop, lanes], ((1,), (0,))))
        context_ref[start:stop, :] = jnp.concatenate(parts, axis=1).astype(BF16)


def attend_back_kernel(qkv_ref, up_ref, grad_ref, bias_ref, total_ref):
    length = qkv_ref.shape[1]
    total_ref[...] = jnp.zeros_like(total_ref)
    bias = jnp.zeros((1, 2 * HEAD), F32)
    for start in range(0, length, ROWS):
        stop = start + ROWS
        parts = []
        for head in range(2):
            lanes = slice(head * HEAD, (head + 1) * HEAD)
            query = qkv_ref[0, start:stop, lanes] * BF16(HEAD**-0.5)
            keys = qkv_ref[1, :stop, lanes]
            values = qkv_ref[2, :stop, lanes]
            upstream = up_ref[start:stop, lanes]
            probs = block_probs(query, keys, start)
            grad_probs = dot(upstream, values, ((1,), (1,)))
            inner = jnp.sum(grad_probs * probs, axis=-1, keepdims=True)
            grad_scores = (probs * (grad_probs - inner)).astype(BF16)
            parts.append(dot(grad_scores, keys, ((1,), (0,))) * (HEAD**-0.5))
            total_ref[0, :stop, lanes] += dot(grad_scores, query, ((0,), (0,)))
            total_ref[1, :stop, lanes] += dot(probs.astype(BF16), upstream, ((0,), (0,)))
        grad_query = jnp.concatenate(parts, axis=1)
        bias = bias + jnp.sum(grad_query, axis=0, keepdims=True)
        grad_ref[0, start:stop, :] = grad_query.astype(BF16)
    grad_ref[1] = total_ref[0].astype(BF16)
    grad_ref[2] = total_ref[1].astype(BF16)
    bias_ref[0] = jnp.broadcast_to(bias, bias_ref.shape[1:])
    bias_ref[1] = jnp.broadcast_to(
        jnp.sum(total_ref[1], axis=0, keepdims=True), bias_ref.shape[1:]
    )


def attend(qkv):
    unused, length, width = qkv.shape
    return pl.pallas_call(
        attend_kernel,
        grid=(width // 128,),
        in_specs=[pl.BlockSpec((3, length, 128), lambda pair: (0, 0, pair))],
        out_specs=pl.BlockSpec((length, 128), lambda pair: (0, pair)),
        out_shape=jax.ShapeDtypeStruct((length, width), BF16),
        compiler_params=pltpu.CompilerParams(vmem_limit_bytes=32 << 20),
        cost_estimate=pl.CostEstimate(
            flops=4 * length * length * width,
            bytes_accessed=8 * length * width,
            transcendentals=length * length * width // HEAD,
        ),
    )(qkv)


def attend_back(qkv, upstream):
    unused, length, width = qkv.shape
    grads, bias = pl.pallas_call(
        attend_back_kernel,
        grid=(width // 128,),
        in_specs=[
            pl.BlockSpec((3, length, 128), lambda pair: (0, 0, pair)),
            pl.BlockSpec((length, 128), lambda pair: (0, pair)),
        ],
        out_specs=(
            pl.BlockSpec((3, length, 128), lambda pair: (0, 0, pair)),
            pl.BlockSpec((2, 8, 128), lambda pair: (0, 0, pair)),
        ),
        out_shape=(
            jax.ShapeDtypeStruct((3, length, width), BF16),
            jax.ShapeDtypeStruct((2, 8, width), F32),
        ),
        scratch_shapes=[pltpu.VMEM((2, length, 128), F32)],
        compiler_params=pltpu.CompilerParams(vmem_limit_bytes=32 << 20),
        cost_estimate=pl.CostEstimate(
            flops=10 * length * length * width,
            bytes_accessed=14 * length * width,
            transcendentals=length * length * width // HEAD,
        ),
    )(qkv, upstream)
    return grads, bias[:, 0]


def to_sequences(rows):
    devices = lax.axis_size("tensor")
    items = rows.transpose(1, 0, 2)
    items = jnp.pad(items, ((0, devices - items.shape[0]), (0, 0), (0, 0)))
    items = lax.all_to_all(items, "tensor", split_axis=0, concat_axis=0, tiled=True)
    return items.reshape(-1, rows.shape[2])


def to_positions(rows, sequences):
    devices = lax.axis_size("tensor")
    items = rows.reshape(devices, -1, rows.shape[1])
    items = lax.all_to_all(items, "tensor", split_axis=0, concat_axis=0, tiled=True)
    return items[:sequences].transpose(1, 0, 2)


def gather(weight, split, head):
    weight = lax.all_gather(weight, "tensor", axis=head, tiled=True)
    return lax.all_gather(weight, "dp", axis=split, tiled=True)


def scatter(grad, split, head):
    grad = lax.psum_scatter(grad.astype(BF16), "dp", scatter_dimension=split, tiled=True)
    grad = lax.psum_scatter(grad, "tensor", scatter_dimension=head, tiled=True)
    return grad.astype(F32)


def on_device(
    inputs,
    cotangent,
    norm_gain,
    norm_shift,
    attention_weight,
    attention_bias,
    output_weight,
    output_bias,
    expand_weight,
    expand_bias,
    contract_weight,
    contract_bias,
):
    sequences = inputs.shape[1]
    layers = attention_weight.shape[0]
    both = ("dp", "tensor")
    small = (norm_gain, norm_shift, attention_bias, output_bias, expand_bias, contract_bias)
    packed = jnp.concatenate([item.reshape(-1) for item in small])
    packed = lax.all_gather(packed, both, axis=0, tiled=False).astype(F32)
    shared = []
    start = 0
    for item in small:
        part = packed[:, start : start + item.size].reshape((-1,) + item.shape)
        shared.append(jnp.moveaxis(part, 0, -2).reshape(item.shape[:-1] + (-1,)))
        start += item.size
    gains, shifts, attention_shift, output_shift, expand_shift, contract_shift = shared
    weights = []
    for layer in range(layers):
        weights.append(
            (
                gather(attention_weight[layer], 1, 2),
                gather(output_weight[layer], 1, 0),
                gather(expand_weight[layer], 0, 1),
                gather(contract_weight[layer], 1, 0),
            )
        )
    residual = to_sequences(inputs).astype(F32)
    width = residual.shape[1]
    stored = []
    for layer in range(layers):
        attention, output, expand, contract = weights[layer]
        scaled, inverse = norm_stats(residual)
        normed = (scaled * gains[layer, 0] + shifts[layer, 0]).astype(BF16)
        shift = jnp.stack(
            [attention_shift[layer, 0], jnp.zeros((width,), F32), attention_shift[layer, 1]]
        )
        qkv = jnp.einsum("ld,cde->cle", normed, attention, preferred_element_type=F32)
        qkv = (qkv + shift[:, None]).astype(BF16)
        context = attend(qkv)
        middle = residual + dot(context, output, ((1,), (0,))) + output_shift[layer]
        scaled, inverse = norm_stats(middle)
        expanded = (scaled * gains[layer, 1] + shifts[layer, 1]).astype(BF16)
        hidden = dot(expanded, expand, ((1,), (0,))) + expand_shift[layer]
        active = smooth_unit(hidden).astype(BF16)
        stored.append((residual, normed, qkv, context, middle, expanded, hidden, active))
        residual = middle + dot(active, contract, ((1,), (0,))) + contract_shift[layer]
    outputs = to_positions(residual.astype(BF16), sequences)
    upstream = to_sequences(cotangent).astype(F32)
    weight_parts = []
    small_parts = []
    for layer in reversed(range(layers)):
        attention, output, expand, contract = weights[layer]
        before, normed, qkv, context, middle, expanded, hidden, active = stored[layer]
        contract_bias_grad = jnp.sum(upstream, axis=0)
        upstream_low = upstream.astype(BF16)
        contract_grad = scatter(dot(active, upstream_low, ((0,), (0,))), 1, 0)
        grad_active = dot(upstream_low, contract, ((1,), (1,)))
        unused, pull_unit = jax.vjp(smooth_unit, hidden)
        grad_hidden = pull_unit(grad_active)[0]
        expand_bias_grad = jnp.sum(grad_hidden, axis=0)
        hidden_low = grad_hidden.astype(BF16)
        expand_grad = scatter(dot(expanded, hidden_low, ((0,), (0,))), 0, 1)
        grad_second = dot(hidden_low, expand, ((1,), (1,)))
        scaled, inverse = norm_stats(middle)
        second_gain = jnp.sum(grad_second * scaled, axis=0)
        second_shift = jnp.sum(grad_second, axis=0)
        grad_middle = upstream + norm_back(grad_second, gains[layer, 1], scaled, inverse)
        output_bias_grad = jnp.sum(grad_middle, axis=0)
        middle_low = grad_middle.astype(BF16)
        output_grad = scatter(dot(context, middle_low, ((0,), (0,))), 1, 0)
        grad_context = dot(middle_low, output, ((1,), (1,))).astype(BF16)
        grad_qkv, attention_bias_grad = attend_back(qkv, grad_context)
        attention_grad = scatter(
            jnp.einsum("ld,cle->cde", normed, grad_qkv, preferred_element_type=F32), 1, 2
        )
        grad_first = jnp.einsum("cle,cde->ld", grad_qkv, attention, preferred_element_type=F32)
        scaled, inverse = norm_stats(before)
        first_gain = jnp.sum(grad_first * scaled, axis=0)
        first_shift = jnp.sum(grad_first, axis=0)
        upstream = grad_middle + norm_back(grad_first, gains[layer, 0], scaled, inverse)
        weight_parts.insert(0, (attention_grad, output_grad, expand_grad, contract_grad))
        small_parts.insert(
            0,
            (
                jnp.stack([first_gain, second_gain]),
                jnp.stack([first_shift, second_shift]),
                attention_bias_grad,
                output_bias_grad,
                expand_bias_grad,
                contract_bias_grad,
            ),
        )
    first_input_grad = to_positions(upstream.astype(BF16), sequences).astype(F32)
    pieces = []
    for index, item in enumerate(small):
        grad = jnp.stack([parts[index] for parts in small_parts])
        grad = grad.reshape(item.shape[:-1] + (-1, item.shape[-1]))
        pieces.append(jnp.moveaxis(grad, -2, 0).reshape(-1, item.size))
    packed = jnp.concatenate(pieces, axis=1)
    packed = lax.psum_scatter(packed, both, scatter_dimension=0, tiled=True)[0]
    small_out = []
    start = 0
    for item in small:
        small_out.append(packed[start : start + item.size].reshape(item.shape))
        start += item.size
    large = [jnp.stack([parts[index] for parts in weight_parts]) for index in range(4)]
    return (
        outputs,
        first_input_grad,
        small_out[0],
        small_out[1],
        large[0],
        small_out[2],
        large[1],
        small_out[3],
        large[2],
        small_out[4],
        large[3],
        small_out[5],
    )


def solution(mesh):
    return jax.shard_map(
        on_device,
        mesh=mesh,
        in_specs=(
            P("tensor", "dp", None),
            P("tensor", "dp", None),
            P(None, None, ("dp", "tensor")),
            P(None, None, ("dp", "tensor")),
            P(None, None, "dp", "tensor"),
            P(None, None, ("dp", "tensor")),
            P(None, "tensor", "dp"),
            P(None, ("dp", "tensor")),
            P(None, "dp", "tensor"),
            P(None, ("dp", "tensor")),
            P(None, "tensor", "dp"),
            P(None, ("dp", "tensor")),
        ),
        out_specs=(
            P("tensor", "dp", None),
            P("tensor", "dp", None),
            P(None, None, ("dp", "tensor")),
            P(None, None, ("dp", "tensor")),
            P(None, None, "dp", "tensor"),
            P(None, None, ("dp", "tensor")),
            P(None, "tensor", "dp"),
            P(None, ("dp", "tensor")),
            P(None, "dp", "tensor"),
            P(None, ("dp", "tensor")),
            P(None, "tensor", "dp"),
            P(None, ("dp", "tensor")),
        ),
        check_vma=False,
    )
```

```python
import functools

import jax
import jax.numpy as jnp
from jax import lax
from jax.experimental import pallas as pl
from jax.experimental.pallas import tpu as pltpu
from jax.sharding import PartitionSpec as P

HEAD = 64
EPSILON = 1e-05
ROWS = 256
F32 = jnp.float32
BF16 = jnp.bfloat16


def norm_stats(rows):
    average = jnp.mean(rows, axis=-1, keepdims=True)
    centred = rows - average
    inverse = lax.rsqrt(jnp.mean(centred * centred, axis=-1, keepdims=True) + EPSILON)
    return (centred * inverse, inverse)


def norm_back(incoming, gain, scaled, inverse):
    weighted = incoming * gain
    first = jnp.mean(weighted, axis=-1, keepdims=True)
    second = jnp.mean(weighted * scaled, axis=-1, keepdims=True)
    return inverse * (weighted - first - scaled * second)


def smooth_unit(values):
    return jax.nn.gelu(values, approximate=True)


def dot(left, right, contract):
    return lax.dot_general(left, right, (contract, ((), ())), preferred_element_type=F32)


def block_probs(query, keys, start):
    scores = dot(query, keys, ((1,), (1,)))
    later = lax.broadcasted_iota(jnp.int32, scores.shape, 0) + start
    earlier = lax.broadcasted_iota(jnp.int32, scores.shape, 1)
    scores = jnp.where(later >= earlier, scores, -1e30)
    powers = jnp.exp(scores - jnp.max(scores, axis=-1, keepdims=True))
    return powers / jnp.sum(powers, axis=-1, keepdims=True)


def attend_kernel(qkv_ref, context_ref):
    length = qkv_ref.shape[1]
    for start in range(0, length, ROWS):
        stop = start + ROWS
        parts = []
        for head in range(2):
            lanes = slice(head * HEAD, (head + 1) * HEAD)
            query = qkv_ref[0, start:stop, lanes] * BF16(HEAD**-0.5)
            probs = block_probs(query, qkv_ref[1, :stop, lanes], start)
            parts.append(dot(probs.astype(BF16), qkv_ref[2, :stop, lanes], ((1,), (0,))))
        context_ref[start:stop, :] = jnp.concatenate(parts, axis=1).astype(BF16)


def attend_back_kernel(qkv_ref, up_ref, grad_ref, bias_ref, total_ref):
    length = qkv_ref.shape[1]
    total_ref[...] = jnp.zeros_like(total_ref)
    bias = jnp.zeros((1, 2 * HEAD), F32)
    for start in range(0, length, ROWS):
        stop = start + ROWS
        parts = []
        for head in range(2):
            lanes = slice(head * HEAD, (head + 1) * HEAD)
            query = qkv_ref[0, start:stop, lanes] * BF16(HEAD**-0.5)
            keys = qkv_ref[1, :stop, lanes]
            values = qkv_ref[2, :stop, lanes]
            upstream = up_ref[start:stop, lanes]
            probs = block_probs(query, keys, start)
            grad_probs = dot(upstream, values, ((1,), (1,)))
            inner = jnp.sum(grad_probs * probs, axis=-1, keepdims=True)
            grad_scores = (probs * (grad_probs - inner)).astype(BF16)
            parts.append(dot(grad_scores, keys, ((1,), (0,))) * (HEAD**-0.5))
            total_ref[0, :stop, lanes] += dot(grad_scores, query, ((0,), (0,)))
            total_ref[1, :stop, lanes] += dot(probs.astype(BF16), upstream, ((0,), (0,)))
        grad_query = jnp.concatenate(parts, axis=1)
        bias = bias + jnp.sum(grad_query, axis=0, keepdims=True)
        grad_ref[0, start:stop, :] = grad_query.astype(BF16)
    grad_ref[1] = total_ref[0].astype(BF16)
    grad_ref[2] = total_ref[1].astype(BF16)
    bias_ref[0] = jnp.broadcast_to(bias, bias_ref.shape[1:])
    bias_ref[1] = jnp.broadcast_to(
        jnp.sum(total_ref[1], axis=0, keepdims=True), bias_ref.shape[1:]
    )


def attend(qkv):
    unused, length, width = qkv.shape
    return pl.pallas_call(
        attend_kernel,
        grid=(width // 128,),
        in_specs=[pl.BlockSpec((3, length, 128), lambda pair: (0, 0, pair))],
        out_specs=pl.BlockSpec((length, 128), lambda pair: (0, pair)),
        out_shape=jax.ShapeDtypeStruct((length, width), BF16),
        compiler_params=pltpu.CompilerParams(vmem_limit_bytes=32 << 20),
        cost_estimate=pl.CostEstimate(
            flops=4 * length * length * width,
            bytes_accessed=8 * length * width,
            transcendentals=length * length * width // HEAD,
        ),
    )(qkv)


def attend_back(qkv, upstream):
    unused, length, width = qkv.shape
    grads, bias = pl.pallas_call(
        attend_back_kernel,
        grid=(width // 128,),
        in_specs=[
            pl.BlockSpec((3, length, 128), lambda pair: (0, 0, pair)),
            pl.BlockSpec((length, 128), lambda pair: (0, pair)),
        ],
        out_specs=(
            pl.BlockSpec((3, length, 128), lambda pair: (0, 0, pair)),
            pl.BlockSpec((2, 8, 128), lambda pair: (0, 0, pair)),
        ),
        out_shape=(
            jax.ShapeDtypeStruct((3, length, width), BF16),
            jax.ShapeDtypeStruct((2, 8, width), F32),
        ),
        scratch_shapes=[pltpu.VMEM((2, length, 128), F32)],
        compiler_params=pltpu.CompilerParams(vmem_limit_bytes=32 << 20),
        cost_estimate=pl.CostEstimate(
            flops=10 * length * length * width,
            bytes_accessed=14 * length * width,
            transcendentals=length * length * width // HEAD,
        ),
    )(qkv, upstream)
    return grads, bias[:, 0]


def to_sequences(rows):
    devices = lax.axis_size("tensor")
    items = rows.transpose(1, 0, 2)
    items = jnp.pad(items, ((0, devices - items.shape[0]), (0, 0), (0, 0)))
    items = lax.all_to_all(items, "tensor", split_axis=0, concat_axis=0, tiled=True)
    return items.reshape(-1, rows.shape[2])


def to_positions(rows, sequences):
    devices = lax.axis_size("tensor")
    items = rows.reshape(devices, -1, rows.shape[1])
    items = lax.all_to_all(items, "tensor", split_axis=0, concat_axis=0, tiled=True)
    return items[:sequences].transpose(1, 0, 2)


def bits_of(axis):
    return [1 << bit for bit in range((lax.axis_size(axis) - 1).bit_length())]


def partner(axis, mask):
    return [(index, index ^ mask) for index in range(lax.axis_size(axis))]


def own_bit(axis, mask):
    return (lax.axis_index(axis) // mask) % 2


def orders(turned):
    masks = bits_of("dp")
    outer = masks[1:][::-1] if turned else masks[1:]
    return outer + masks[:1]


def join_step(array, axis, mask, place):
    other = lax.ppermute(array, axis, partner(axis, mask))
    low = own_bit(axis, mask) == 0
    first, second = jnp.where(low, array, other), jnp.where(low, other, array)
    return jnp.stack([first, second], axis=place)


def halve_step(array, axis, mask, place):
    bit = own_bit(axis, mask)
    kept = lax.dynamic_index_in_dim(array, bit, place, keepdims=False)
    sent = lax.dynamic_index_in_dim(array, 1 - bit, place, keepdims=False)
    arrived = lax.ppermute(sent, axis, partner(axis, mask))
    return (kept.astype(F32) + arrived.astype(F32)).astype(array.dtype)


def gather(weight, turned):
    lead = weight.ndim - 2
    for mask in bits_of("tensor"):
        weight = join_step(weight, "tensor", mask, 0)
    parts = lax.axis_size("tensor")
    weight = weight.reshape((parts,) + weight.shape[-2 - lead :])
    weight = jnp.moveaxis(weight, 0, -2)
    weight = weight.reshape(weight.shape[:-2] + (-1,))
    held = []
    for mask in orders(turned):
        place = sum(1 for other in held if other > mask)
        held.append(mask)
        weight = join_step(weight, "dp", mask, lead + place)
    return weight.reshape(weight.shape[:lead] + (-1, weight.shape[-1]))


def scatter(grad, turned):
    lead = grad.ndim - 2
    grad = grad.astype(BF16)
    masks = bits_of("dp")
    rows = grad.shape[lead] >> len(masks)
    grad = grad.reshape(grad.shape[:lead] + (2,) * len(masks) + (rows, grad.shape[-1]))
    held = masks
    for mask in orders(turned)[::-1]:
        place = sum(1 for other in held if other > mask)
        held = [other for other in held if other != mask]
        grad = halve_step(grad, "dp", mask, lead + place)
    parts = lax.axis_size("tensor")
    grad = grad.reshape(grad.shape[:-1] + (parts, -1))
    grad = jnp.moveaxis(grad, -2, 0)
    grad = grad.reshape((2,) * len(bits_of("tensor")) + grad.shape[1:])
    for mask in bits_of("tensor")[::-1]:
        grad = halve_step(grad, "tensor", mask, 0)
    return grad.astype(F32)


def gather_small(packed):
    packed = packed[None]
    for axis in ("tensor", "dp"):
        for mask in bits_of(axis):
            packed = join_step(packed, axis, mask, 0)
            packed = packed.reshape((-1,) + packed.shape[2:])
    return packed


def scatter_small(packed):
    for axis in ("dp", "tensor"):
        for mask in bits_of(axis)[::-1]:
            packed = packed.reshape((2, -1) + packed.shape[1:])
            packed = halve_step(packed, axis, mask, 0)
    return packed[0]


def on_device(
    inputs,
    cotangent,
    norm_gain,
    norm_shift,
    attention_weight,
    attention_bias,
    output_weight,
    output_bias,
    expand_weight,
    expand_bias,
    contract_weight,
    contract_bias,
):
    sequences = inputs.shape[1]
    layers = attention_weight.shape[0]
    small = (norm_gain, norm_shift, attention_bias, output_bias, expand_bias, contract_bias)
    packed = jnp.concatenate([item.reshape(-1) for item in small])
    packed = gather_small(packed).astype(F32)
    shared = []
    start = 0
    for item in small:
        part = packed[:, start : start + item.size].reshape((-1,) + item.shape)
        shared.append(jnp.moveaxis(part, 0, -2).reshape(item.shape[:-1] + (-1,)))
        start += item.size
    gains, shifts, attention_shift, output_shift, expand_shift, contract_shift = shared
    weights = []
    for layer in range(layers):
        weights.append(
            (
                gather(attention_weight[layer], layer % 2 == 1),
                gather(output_weight[layer].T, layer % 2 == 0),
                gather(expand_weight[layer], False),
                gather(contract_weight[layer].T, True),
            )
        )
    residual = to_sequences(inputs).astype(F32)
    width = residual.shape[1]
    stored = []
    for layer in range(layers):
        attention, output, expand, contract = weights[layer]
        scaled, inverse = norm_stats(residual)
        normed = (scaled * gains[layer, 0] + shifts[layer, 0]).astype(BF16)
        shift = jnp.stack(
            [attention_shift[layer, 0], jnp.zeros((width,), F32), attention_shift[layer, 1]]
        )
        qkv = jnp.einsum("ld,cde->cle", normed, attention, preferred_element_type=F32)
        qkv = (qkv + shift[:, None]).astype(BF16)
        context = attend(qkv)
        middle = residual + dot(context, output, ((1,), (1,))) + output_shift[layer]
        scaled, inverse = norm_stats(middle)
        expanded = (scaled * gains[layer, 1] + shifts[layer, 1]).astype(BF16)
        hidden = dot(expanded, expand, ((1,), (0,))) + expand_shift[layer]
        active = smooth_unit(hidden).astype(BF16)
        stored.append((residual, normed, qkv, context, middle, expanded, hidden, active))
        residual = middle + dot(active, contract, ((1,), (1,))) + contract_shift[layer]
    outputs = to_positions(residual.astype(BF16), sequences)
    upstream = to_sequences(cotangent).astype(F32)
    weight_parts = []
    small_parts = []
    for layer in reversed(range(layers)):
        attention, output, expand, contract = weights[layer]
        before, normed, qkv, context, middle, expanded, hidden, active = stored[layer]
        contract_bias_grad = jnp.sum(upstream, axis=0)
        upstream_low = upstream.astype(BF16)
        contract_grad = scatter(dot(upstream_low, active, ((0,), (0,))), True).T
        grad_active = dot(upstream_low, contract, ((1,), (0,)))
        unused, pull_unit = jax.vjp(smooth_unit, hidden)
        grad_hidden = pull_unit(grad_active)[0]
        expand_bias_grad = jnp.sum(grad_hidden, axis=0)
        hidden_low = grad_hidden.astype(BF16)
        expand_grad = scatter(dot(expanded, hidden_low, ((0,), (0,))), False)
        grad_second = dot(hidden_low, expand, ((1,), (1,)))
        scaled, inverse = norm_stats(middle)
        second_gain = jnp.sum(grad_second * scaled, axis=0)
        second_shift = jnp.sum(grad_second, axis=0)
        grad_middle = upstream + norm_back(grad_second, gains[layer, 1], scaled, inverse)
        output_bias_grad = jnp.sum(grad_middle, axis=0)
        middle_low = grad_middle.astype(BF16)
        output_grad = scatter(dot(middle_low, context, ((0,), (0,))), layer % 2 == 0).T
        grad_context = dot(middle_low, output, ((1,), (0,))).astype(BF16)
        grad_qkv, attention_bias_grad = attend_back(qkv, grad_context)
        attention_grad = scatter(
            jnp.einsum("ld,cle->cde", normed, grad_qkv, preferred_element_type=F32), layer % 2 == 1
        )
        grad_first = jnp.einsum("cle,cde->ld", grad_qkv, attention, preferred_element_type=F32)
        scaled, inverse = norm_stats(before)
        first_gain = jnp.sum(grad_first * scaled, axis=0)
        first_shift = jnp.sum(grad_first, axis=0)
        upstream = grad_middle + norm_back(grad_first, gains[layer, 0], scaled, inverse)
        weight_parts.insert(0, (attention_grad, output_grad, expand_grad, contract_grad))
        small_parts.insert(
            0,
            (
                jnp.stack([first_gain, second_gain]),
                jnp.stack([first_shift, second_shift]),
                attention_bias_grad,
                output_bias_grad,
                expand_bias_grad,
                contract_bias_grad,
            ),
        )
    first_input_grad = to_positions(upstream.astype(BF16), sequences).astype(F32)
    pieces = []
    for index, item in enumerate(small):
        grad = jnp.stack([parts[index] for parts in small_parts])
        grad = grad.reshape(item.shape[:-1] + (-1, item.shape[-1]))
        pieces.append(jnp.moveaxis(grad, -2, 0).reshape(-1, item.size))
    packed = jnp.concatenate(pieces, axis=1)
    packed = scatter_small(packed)
    small_out = []
    start = 0
    for item in small:
        small_out.append(packed[start : start + item.size].reshape(item.shape))
        start += item.size
    large = [jnp.stack([parts[index] for parts in weight_parts]) for index in range(4)]
    return (
        outputs,
        first_input_grad,
        small_out[0],
        small_out[1],
        large[0],
        small_out[2],
        large[1],
        small_out[3],
        large[2],
        small_out[4],
        large[3],
        small_out[5],
    )


def solution(mesh):
    return jax.shard_map(
        on_device,
        mesh=mesh,
        in_specs=(
            P("tensor", "dp", None),
            P("tensor", "dp", None),
            P(None, None, ("dp", "tensor")),
            P(None, None, ("dp", "tensor")),
            P(None, None, "dp", "tensor"),
            P(None, None, ("dp", "tensor")),
            P(None, "tensor", "dp"),
            P(None, ("dp", "tensor")),
            P(None, "dp", "tensor"),
            P(None, ("dp", "tensor")),
            P(None, "tensor", "dp"),
            P(None, ("dp", "tensor")),
        ),
        out_specs=(
            P("tensor", "dp", None),
            P("tensor", "dp", None),
            P(None, None, ("dp", "tensor")),
            P(None, None, ("dp", "tensor")),
            P(None, None, "dp", "tensor"),
            P(None, None, ("dp", "tensor")),
            P(None, "tensor", "dp"),
            P(None, ("dp", "tensor")),
            P(None, "dp", "tensor"),
            P(None, ("dp", "tensor")),
            P(None, "tensor", "dp"),
            P(None, ("dp", "tensor")),
        ),
        check_vma=False,
    )
```
